32 devices in a mesh: box: 16 (over z, y, x), row: 2 (over core).
Axes of the slice: x: 2, y: 2, z: 4, core: 2. Of those that a mesh axis runs over, the one named last changes fastest.
Arguments:
- rhs: float32 [128, 64, 320], P('box'), may hold values from -6 to 6
- skel1: int32 [128, 192], P('box'), may hold values from 0 to 319, as said below
- red1: int32 [128, 128], P('box'), may hold values from 0 to 319, as said below
- interp1: bfloat16 [128, 128, 192], P('box', None, 'row'), may hold values from -0.5 to 0.5
- inv1: bfloat16 [128, 128, 128], P('box', None, 'row'), may hold values from -0.5 to 0.5
- couple1: bfloat16 [128, 8, 128, 192], P('box', None, None, 'row'), may hold values from -0.5 to 0.5
- near1: int32 [128, 8], P('box'), may hold values from -1 to 127, as said below
- skel2: int32 [16, 384], P('box'), may hold values from 0 to 1535, as said below
- red2: int32 [16, 1152], P('box'), may hold values from 0 to 1535, as said below
- interp2: bfloat16 [16, 1152, 384], P('box', None, 'row'), may hold values from -0.1875 to 0.1875
- inv2: bfloat16 [16, 1152, 1152], P('box', None, 'row'), may hold values from -0.1875 to 0.1875
- panel2: bfloat16 [16, 2, 1152, 384], P('box', None, None, 'row'), may hold values from -0.1875 to 0.1875
- near2: int32 [16, 2], P('box'), may hold values from -1 to 15, as said below
Outputs:
- red_one: float32 [128, 64, 128], P('box', None, 'row')
- red_two: float32 [16, 64, 1152], P('box', None, 'row')
- skel_two: float32 [16, 64, 384], P('box', None, 'row')
The draws below stay inside these ranges and needn't reach their ends.
Inputs may be any that keep to these rules, and one draw needn't show every extreme that they name: For each leaf box, skel1 and red1 together hold every number below 320 exactly once. `red1`: see skel1. For each parent box, skel2 and red2 together hold every number below 1536 exactly once. `red2`: see skel2. `near1`: an entry of box b is -1 or another leaf box c with |c // 8 - b // 8| <= 2; a box may be named twice. `near2`: slot 0 of parent q is q - 1 or -1, slot 1 is q + 1 or -1.
All inputs are finite; a program needn't handle non-finite values.
Results may differ from the reference program's by a relative error of at most 0.0046.
Values may be sent and summed in bfloat16 or wider, within the bound.
No kernel may reach another device: no remote copies, remote signals or barrier semaphores. Data moves between devices by JAX's collectives and lax.ppermute only.
A program may use at most 64 MiB of HBM per device.

```python
import jax
import jax.numpy as jnp
from jax import lax

S1 = 192
R1 = 128
NDOF = 320
CHILD = 8
S2 = 384
R2 = 1152
NB1 = 8
NB2 = 2
K = 64
NBOX = 128
NPAR = 16


def split_lists(key, boxes, total, keep):
    base = jax.random.fold_in(key, 11)
    keys = jax.random.split(base, boxes)
    orders = jax.vmap(lambda sub: jax.random.permutation(sub, total))(keys)
    orders = orders.astype(jnp.int32)
    return (orders[:, :keep], orders[:, keep:])


def draw_skel1(key, part):
    return split_lists(key, NBOX, NDOF, S1)[0]


def draw_red1(key, part):
    return split_lists(key, NBOX, NDOF, S1)[1]


def draw_skel2(key, part):
    return split_lists(jax.random.fold_in(key, 5), NPAR, CHILD * S1, S2)[0]


def draw_red2(key, part):
    return split_lists(jax.random.fold_in(key, 5), NPAR, CHILD * S1, S2)[1]


def draw_near1(key, part):
    base = jax.random.fold_in(key, 21)
    step_key, keep_key = jax.random.split(base)
    boxes = jnp.arange(NBOX, dtype=jnp.int32)[:, None]
    step = jax.random.randint(step_key, (NBOX, NB1), -2 * CHILD, 3 * CHILD, dtype=jnp.int32)
    target = boxes // CHILD * CHILD + step
    keep = jax.random.randint(keep_key, (NBOX, NB1), 0, 4, dtype=jnp.int32) > 0
    good = keep & (target >= 0) & (target < NBOX) & (target != boxes)
    near = jnp.where(good, target, -1).astype(jnp.int32)
    near = near.at[NBOX - 2, 0].set(NBOX - 1)
    near = near.at[0, NB1 - 1].set(-1)
    return near.astype(jnp.int32)


def draw_near2(key, part):
    base = jax.random.fold_in(key, 31)
    parents = jnp.arange(NPAR, dtype=jnp.int32)[:, None]
    target = parents + jnp.array([[-1, 1]], dtype=jnp.int32)
    keep = jax.random.randint(base, (NPAR, NB2), 0, 4, dtype=jnp.int32) > 0
    good = keep & (target >= 0) & (target < NPAR)
    near = jnp.where(good, target, -1).astype(jnp.int32)
    near = near.at[NPAR - 2, 1].set(NPAR - 1)
    return near.astype(jnp.int32)


def steps_of(key, shape, cuts, low, top_value):
    factor_of = 1.0
    for axis_at, parts in cuts:
        heights = jax.random.uniform(jax.random.fold_in(jax.random.fold_in(key, 6), axis_at), (parts,), jnp.float32, low / len(cuts), top_value / len(cuts))
        factor_of = factor_of * jnp.repeat(jnp.exp(heights), shape[axis_at] // parts).reshape((-1,) + (1,) * (len(shape) - 1 - axis_at))
    return factor_of


def gaussian(stream_key, dims, spread, limit, cuts=(), held_as=jnp.bfloat16):
    gain = steps_of(stream_key, dims, cuts, -0.22, 0.18) if cuts else 1.0
    values = jax.random.normal(stream_key, dims, jnp.float32) * spread * gain
    return jnp.minimum(jnp.maximum(values, -limit), limit).astype(held_as)


def setup_inputs(seed: int = 0) -> dict:
    streams_of = jax.random.split(jax.random.key(seed), 14)
    rhs = gaussian(streams_of[0], (NBOX, K, NDOF), 1.0, 6.0, ((0, 16),), jnp.float32)
    skel1 = draw_skel1(jax.random.fold_in(streams_of[13], 71), 0)
    red1 = draw_red1(jax.random.fold_in(streams_of[13], 71), 0)
    interp1 = gaussian(streams_of[3], (NBOX, R1, S1), R1 ** -0.5, 0.5, ((0, 16), (2, 2)))
    inv1 = gaussian(streams_of[4], (NBOX, R1, R1), R1 ** -0.5, 0.5, ((0, 16), (2, 2)))
    couple1 = gaussian(streams_of[5], (NBOX, NB1, R1, S1), R1 ** -0.5, 0.5, ((0, 16), (3, 2)))
    near1 = draw_near1(jax.random.fold_in(streams_of[13], 71), 0)
    skel2 = draw_skel2(jax.random.fold_in(streams_of[13], 71), 0)
    red2 = draw_red2(jax.random.fold_in(streams_of[13], 71), 0)
    interp2 = gaussian(streams_of[9], (NPAR, R2, S2), R2 ** -0.5, 0.1875, ((0, 16), (2, 2)))
    inv2 = gaussian(streams_of[10], (NPAR, R2, R2), R2 ** -0.5, 0.1875, ((0, 16), (2, 2)))
    panel2 = gaussian(streams_of[11], (NPAR, NB2, R2, S2), R2 ** -0.5, 0.1875, ((0, 16), (3, 2)))
    near2 = draw_near2(jax.random.fold_in(streams_of[13], 71), 0)
    return {"rhs": rhs, "skel1": skel1, "red1": red1, "interp1": interp1, "inv1": inv1, "couple1": couple1, "near1": near1, "skel2": skel2, "red2": red2, "interp2": interp2, "inv2": inv2, "panel2": panel2, "near2": near2}


def pick(values, index):
    return jax.vmap(lambda block, where: block[:, where])(values, index)


def route_sum(updates, near, count):
    targets = jnp.where(near >= 0, near, count).reshape(-1)
    flat = updates.reshape((-1,) + updates.shape[2:])
    summed = jax.ops.segment_sum(flat, targets, num_segments=count + 1)
    return summed[:count]


def reference(rhs, skel1, red1, interp1, inv1, couple1, near1, skel2, red2, interp2, inv2, panel2, near2):
    high = lax.Precision.HIGHEST
    xr1 = pick(rhs, red1).astype(jnp.bfloat16).astype(jnp.float32)
    ys1 = pick(rhs, skel1) - jnp.einsum("bkr,brs->bks", xr1, interp1.astype(jnp.float32), precision=high)
    red_one = jnp.einsum("bkr,brq->bkq", xr1, inv1.astype(jnp.float32), precision=high)
    w1 = red_one.astype(jnp.bfloat16).astype(jnp.float32)
    u1 = jnp.einsum("bkr,bjrs->bjks", w1, couple1.astype(jnp.float32), precision=high)
    z1 = ys1 + route_sum(u1, near1, NBOX)
    parent = z1.reshape(NPAR, CHILD, K, S1).transpose(0, 2, 1, 3).reshape(NPAR, K, CHILD * S1)
    xr2 = pick(parent, red2).astype(jnp.bfloat16).astype(jnp.float32)
    ys2 = pick(parent, skel2) - jnp.einsum("pkr,prs->pks", xr2, interp2.astype(jnp.float32), precision=high)
    red_two = jnp.einsum("pkr,prq->pkq", xr2, inv2.astype(jnp.float32), precision=high)
    u2 = jnp.einsum("pkr,pjrs->pjks", xr2, panel2.astype(jnp.float32), precision=high)
    skel_two = ys2 + route_sum(u2, near2, NPAR)
    return red_one, red_two, skel_two
```

```python
import functools

import jax
import jax.numpy as jnp
from jax import lax
from jax.experimental import pallas as pl
from jax.experimental.pallas import tpu as pltpu
from jax.sharding import PartitionSpec as P

F32 = jnp.float32
BF16 = jnp.bfloat16
REACH = 2


def row_pieces(block):
    rows = lax.axis_size("row")
    others = [
        lax.ppermute(block, "row", [(i, i ^ t) for i in range(rows)]) for t in range(1, rows)
    ]
    return [block] + others


def box_permute(block, distance, flip):
    boxes, rows = lax.axis_size("box"), lax.axis_size("row")
    route = []
    for box in range(boxes):
        for row in range(rows):
            target = box + (distance if (row % 2 == 0) != flip else -distance)
            inside = 0 <= target < boxes
            place = target * rows + row if inside else box * rows + (row ^ 1)
            route.append((box * rows + row, place))
    return lax.ppermute(block, ("box", "row"), route)


def onehot(index, count, dtype=BF16):
    spots = lax.broadcasted_iota(jnp.int32, (count, index.shape[1]), 0)
    return jnp.where(spots == index, 1.0, 0.0).astype(dtype)


def dot(a, b):
    return jnp.dot(a, b, preferred_element_type=F32)


def dot_t(a, b):
    return lax.dot_general(a, b, (((1,), (1,)), ((), ())), preferred_element_type=F32)


def turned(panel):
    return jnp.swapaxes(panel, -1, -2)


def own_part(values, block):
    row = lax.axis_index("row")
    chosen = values[:, :block]
    for place in range(1, values.shape[1] // block):
        part = values[:, place * block : (place + 1) * block]
        chosen = jnp.where(row == place, part, chosen)
    return chosen


def call(body, out_shape, scratch=(), vmem=48 << 20, flops=0, size=0):
    return pl.pallas_call(
        body,
        out_shape=out_shape,
        scratch_shapes=list(scratch),
        compiler_params=pltpu.CompilerParams(vmem_limit_bytes=vmem),
        cost_estimate=pl.CostEstimate(flops=flops, bytes_accessed=size, transcendentals=0),
    )


def struct(shape, dtype):
    return jax.ShapeDtypeStruct(shape, dtype)


def pick_kernel(
    rhs, red, skel, interp, couple, inv, xr_out, ys_out, couple_out, inv_out,
    rhs_in, red_in, skel_in, interp_in, sems,
):
    groups, columns, total = rhs.shape
    block = interp.shape[1]
    ahead = [
        pltpu.make_async_copy(source, held, sems.at[groups + i])
        for i, (source, held) in enumerate(
            ((red, red_in), (skel, skel_in), (interp, interp_in), (inv, inv_out))
        )
    ]
    ahead += [
        pltpu.make_async_copy(couple.at[g], couple_out.at[g], sems.at[groups + 4 + g])
        for g in range(groups)
    ]
    boxes = [pltpu.make_async_copy(rhs.at[g], rhs_in.at[g], sems.at[g]) for g in range(groups)]
    for copy in ahead[:2] + boxes + ahead[2:]:
        copy.start()
    for copy in ahead[:2] + boxes + ahead[2:3]:
        copy.wait()
    own = own_part(skel_in[...], block)
    for g in range(groups):
        whole = rhs_in[g]
        high = whole.astype(BF16)
        low = (whole - high.astype(F32)).astype(BF16)
        xr = dot(high, onehot(red_in[g : g + 1, :], total)).astype(BF16)
        xr_out[g] = xr
        spots = onehot(own[g : g + 1, :], total)
        both = dot(jnp.concatenate([high, low], axis=0), spots)
        ys = both[:columns] + both[columns:] - dot_t(xr, interp_in[g])
        ys_out[:, g * block : (g + 1) * block] = ys
    for copy in ahead[3:]:
        copy.wait()


def leaf_kernel(rows, near, xr, ys, *refs):
    inv = refs[:rows]
    couple, red_out, own_out = refs[rows : rows + 3]
    sends = refs[rows + 3 : rows + 3 + 2 * REACH]
    acc = refs[-1]
    groups, slots = near.shape
    block = couple.shape[2]
    row = lax.axis_index("row")
    anchor = lax.axis_index("box")
    sign = 1 - 2 * (row % 2)
    acc[...] = jnp.zeros_like(acc)
    leaves = []
    for g in range(groups):
        parts = [dot_t(xr[g], inv[t][g]) for t in range(rows)]
        red_out[g] = parts[0]
        placed = []
        for place in range(rows):
            chosen = parts[0]
            for t in range(1, rows):
                chosen = jnp.where(row == (place ^ t), parts[t], chosen)
            placed.append(chosen)
        leaves.append(jnp.concatenate(placed, axis=1).astype(BF16))
    for g in range(groups):
        updates = dot_t(leaves[g], couple[g].reshape(slots * block, couple.shape[3]))
        for j in range(slots):
            target = near[g, j]
            clear = jnp.maximum(target, 0)
            section = (clear // groups - anchor) * sign + REACH
            spot = jnp.where(target >= 0, section * groups + clear % groups, acc.shape[0] - 1)
            acc[spot] += updates[:, j * block : (j + 1) * block]

    def merged(section):
        return jnp.concatenate([acc[section * groups + g] for g in range(groups)], axis=1)

    own_out[...] = ys[...] + merged(REACH)
    for ref, section in zip(sends, SECTIONS):
        ref[...] = merged(section + REACH).astype(BF16)


SECTIONS = (1, -1, 2, -2)


def sum_kernel(*refs):
    total = refs[0][...]
    for ref in refs[1:-2]:
        total = total + ref[...].astype(F32)
    refs[-2][...] = total
    refs[-1][...] = total.astype(BF16)


def shifted_index(index, half, rows, block, groups, skeletons):
    child, place = index // skeletons, index % skeletons
    piece = (place // block) ^ half
    return piece * (groups * block) + child * block + place % block


def parent_kernel(rows, near, red, *refs):
    pieces = refs[:rows]
    panel, xr_out = refs[rows : rows + 2]
    sends = refs[rows + 2 :]
    width = pieces[0].shape[1]
    redundant = red.shape[1]
    step = 128
    parent = jnp.concatenate([ref[...] for ref in pieces], axis=1)
    for start in range(0, redundant, step):
        stop = min(start + step, redundant)
        spots = onehot(red[:, start:stop], rows * width)
        xr_out[:, start:stop] = dot(parent, spots).astype(BF16)
    xr = xr_out[...]
    down = lax.axis_index("row") % 2
    for send, slot in zip(sends, (1 - down, down)):
        update = dot_t(xr, panel[0, slot])
        send[...] = jnp.where(near[0, slot] >= 0, update, 0.0).astype(BF16)


def finish_kernel(rows, skel, xr, interp, inv, own, *refs):
    pieces = refs[: rows - 1]
    red_out, ys_out = refs[rows - 1 :]
    width = own.shape[1]
    red_out[0] = dot_t(xr[...], inv[0])
    high = own[...].astype(BF16)
    low = (own[...] - high.astype(F32)).astype(BF16)
    spots = onehot(skel[...], rows * width)
    picked = dot(jnp.concatenate([high] + [ref[...] for ref in pieces], axis=1), spots)
    picked = picked + dot(low, spots[:width])
    ys_out[0] = picked - dot_t(xr[...], interp[0])


def shards(
    rhs, skel1, red1, interp1, inv1, couple1, near1, skel2, red2, interp2, inv2, panel2, near2
):
    rows = lax.axis_size("row")
    row = lax.axis_index("row")
    groups, columns, total = rhs.shape
    redundant, block = interp1.shape[1:]
    skeletons = skel1.shape[1]
    width = groups * block
    s2_block, i2_block = interp2.shape[2], inv2.shape[2]
    red2_count = red2.shape[1]

    inverse = row_pieces(turned(inv1))[1:]
    hbm = pl.BlockSpec(memory_space=pltpu.HBM)
    inv1, interp1, couple1 = turned(inv1), turned(interp1), turned(couple1)
    xr1, ys1, couple1, own_inv1 = pl.pallas_call(
        pick_kernel,
        out_shape=(
            struct((groups, columns, redundant), BF16),
            struct((columns, width), F32),
            struct(couple1.shape, BF16),
            struct(inv1.shape, BF16),
        ),
        in_specs=[hbm] * 6,
        scratch_shapes=[
            pltpu.VMEM(rhs.shape, F32),
            pltpu.VMEM(red1.shape, jnp.int32),
            pltpu.VMEM(skel1.shape, jnp.int32),
            pltpu.VMEM(interp1.shape, BF16),
            pltpu.SemaphoreType.DMA((2 * groups + 4,)),
        ],
        compiler_params=pltpu.CompilerParams(vmem_limit_bytes=48 << 20),
    )(*(pltpu.with_memory_space_constraint(v, pltpu.HBM) for v in (rhs, red1, skel1, interp1, couple1, inv1)))

    vmem = pl.BlockSpec(memory_space=pltpu.VMEM)
    red_one, own, *sends = pl.pallas_call(
        functools.partial(leaf_kernel, rows),
        out_shape=(
            struct((groups, columns, inv1.shape[1]), F32),
            struct((columns, width), F32),
        )
        + tuple(struct((columns, width), BF16) for _ in SECTIONS),
        in_specs=[pl.BlockSpec(memory_space=pltpu.SMEM)] + [vmem] * (rows + 3),
        scratch_shapes=[pltpu.VMEM(((2 * REACH + 1) * groups + 1, columns, block), F32)],
        compiler_params=pltpu.CompilerParams(vmem_limit_bytes=48 << 20),
    )(near1, xr1, ys1, own_inv1, *inverse, couple1)

    arrived = [
        box_permute(block_, abs(section), section < 0)
        for block_, section in zip(sends, SECTIONS)
    ]
    own_sum, own_high = call(
        sum_kernel, (struct((columns, width), F32), struct((columns, width), BF16))
    )(own, *arrived)
    pieces = row_pieces(own_high)

    place2 = functools.partial(
        shifted_index, half=row, rows=rows, block=block, groups=groups, skeletons=skeletons
    )
    own_skel2 = lax.dynamic_slice_in_dim(skel2, row * s2_block, s2_block, 1)
    xr2, send_up, send_down = pl.pallas_call(
        functools.partial(parent_kernel, rows),
        out_shape=(struct((columns, red2_count), BF16),)
        + tuple(struct((columns, s2_block), BF16) for _ in range(2)),
        in_specs=[pl.BlockSpec(memory_space=pltpu.SMEM)] + [vmem] * (rows + 2),
        compiler_params=pltpu.CompilerParams(vmem_limit_bytes=48 << 20),
    )(near2, place2(red2), *pieces, turned(panel2))
    moved = [box_permute(send_up, 1, False), box_permute(send_down, 1, True)]
    red_two, ys2 = call(
        functools.partial(finish_kernel, rows),
        (struct((1, columns, i2_block), F32), struct((1, columns, s2_block), F32)),
    )(place2(own_skel2), xr2, turned(interp2), turned(inv2), own_sum, *pieces[1:])
    skel_two = ys2 + moved[0].astype(F32)[None] + moved[1].astype(F32)[None]
    return red_one, red_two, skel_two


def solution(mesh):
    return jax.shard_map(
        shards,
        mesh=mesh,
        in_specs=(
            P("box", None, None),
            P("box", None),
            P("box", None),
            P("box", None, "row"),
            P("box", None, "row"),
            P("box", None, None, "row"),
            P("box", None),
            P("box", None),
            P("box", None),
            P("box", None, "row"),
            P("box", None, "row"),
            P("box", None, None, "row"),
            P("box", None),
        ),
        out_specs=(P("box", None, "row"), P("box", None, "row"), P("box", None, "row")),
        check_vma=False,
    )
```

```python
import functools

import jax
import jax.numpy as jnp
from jax import lax
from jax.experimental import pallas as pl
from jax.experimental.pallas import tpu as pltpu
from jax.sharding import PartitionSpec as P

F32 = jnp.float32
BF16 = jnp.bfloat16
REACH = 2


def row_pieces(block):
    rows = lax.axis_size("row")
    others = [
        lax.ppermute(block, "row", [(i, i ^ t) for i in range(rows)]) for t in range(1, rows)
    ]
    return [block] + others


def box_permute(block, distance, flip):
    boxes, rows = lax.axis_size("box"), lax.axis_size("row")
    route = []
    for box in range(boxes):
        for row in range(rows):
            target = box + (distance if (row % 2 == 0) != flip else -distance)
            inside = 0 <= target < boxes
            place = target * rows + row if inside else box * rows + (row ^ 1)
            route.append((box * rows + row, place))
    return lax.ppermute(block, ("box", "row"), route)


def onehot(index, count, dtype=BF16):
    spots = lax.broadcasted_iota(jnp.int32, (count, index.shape[1]), 0)
    return jnp.where(spots == index, 1.0, 0.0).astype(dtype)


def dot(a, b):
    return jnp.dot(a, b, preferred_element_type=F32)


def dot_t(a, b):
    return lax.dot_general(a, b, (((1,), (1,)), ((), ())), preferred_element_type=F32)


def turned(panel):
    return jnp.swapaxes(panel, -1, -2)


def own_part(values, block):
    row = lax.axis_index("row")
    chosen = values[:, :block]
    for place in range(1, values.shape[1] // block):
        part = values[:, place * block : (place + 1) * block]
        chosen = jnp.where(row == place, part, chosen)
    return chosen


def struct(shape, dtype):
    return jax.ShapeDtypeStruct(shape, dtype)


def pick_kernel(
    rhs, red, skel, interp, couple, inv, xr_out, ys_out, couple_out, inv_out,
    rhs_in, red_in, skel_in, interp_in, sems,
):
    groups, columns, total = rhs.shape
    block = interp.shape[1]
    ahead = [
        pltpu.make_async_copy(source, held, sems.at[groups + i])
        for i, (source, held) in enumerate(
            ((red, red_in), (skel, skel_in), (interp, interp_in), (inv, inv_out))
        )
    ]
    ahead += [
        pltpu.make_async_copy(couple.at[g], couple_out.at[g], sems.at[groups + 4 + g])
        for g in range(groups)
    ]
    boxes = [pltpu.make_async_copy(rhs.at[g], rhs_in.at[g], sems.at[g]) for g in range(groups)]
    for copy in ahead[:2] + boxes + ahead[2:]:
        copy.start()
    for copy in ahead[:2] + boxes + ahead[2:3]:
        copy.wait()
    own = own_part(skel_in[...], block)
    for g in range(groups):
        whole = rhs_in[g]
        high = whole.astype(BF16)
        low = (whole - high.astype(F32)).astype(BF16)
        xr = dot(high, onehot(red_in[g : g + 1, :], total)).astype(BF16)
        xr_out[g] = xr
        spots = onehot(own[g : g + 1, :], total)
        both = dot(jnp.concatenate([high, low], axis=0), spots)
        ys = both[:columns] + both[columns:] - dot_t(xr, interp_in[g])
        ys_out[:, g * block : (g + 1) * block] = ys
    for copy in ahead[3:]:
        copy.wait()


def leaf_kernel(rows, near_held, xr, ys, *refs):
    inv = refs[:rows]
    couple, own_out = refs[rows : rows + 2]
    sends = refs[rows + 2 : rows + 2 + 2 * REACH]
    acc, near, sem = refs[-3:]
    fetch = pltpu.make_async_copy(near_held, near, sem)
    fetch.start()
    groups, slots = near.shape
    block = couple.shape[2]
    row = lax.axis_index("row")
    anchor = lax.axis_index("box")
    sign = 1 - 2 * (row % 2)
    acc[...] = jnp.zeros_like(acc)
    leaves = []
    for g in range(groups):
        parts = [dot_t(xr[g], inv[t][g]) for t in range(rows)]
        placed = []
        for place in range(rows):
            chosen = parts[0]
            for t in range(1, rows):
                chosen = jnp.where(row == (place ^ t), parts[t], chosen)
            placed.append(chosen)
        leaves.append(jnp.concatenate(placed, axis=1).astype(BF16))
    fetch.wait()
    for g in range(groups):
        updates = dot_t(leaves[g], couple[g].reshape(slots * block, couple.shape[3]))
        for j in range(slots):
            target = near[g, j]
            clear = jnp.maximum(target, 0)
            section = (clear // groups - anchor) * sign + REACH
            spot = jnp.where(target >= 0, section * groups + clear % groups, acc.shape[0] - 1)
            acc[spot] += updates[:, j * block : (j + 1) * block]

    def merged(section):
        return jnp.concatenate([acc[section * groups + g] for g in range(groups)], axis=1)

    own_out[...] = ys[...] + merged(REACH)
    for ref, section in zip(sends, SECTIONS):
        ref[...] = merged(section + REACH).astype(BF16)


SECTIONS = (1, -1, 2, -2)


def shifted_index(index, half, block, groups, skeletons):
    child, place = index // skeletons, index % skeletons
    piece = (place // block) ^ half
    return piece * (groups * block) + child * block + place % block


def spread_kernel(near, red, panel, xr, inv1, red_out, out):
    for g in range(xr.shape[0]):
        red_out[g] = dot_t(xr[g], inv1[g])
    spots = onehot(red[...], out.shape[1])
    for slot in range(out.shape[0]):
        spread = dot_t(spots, panel[0, slot])
        out[slot] = jnp.where(near[0, slot] >= 0, spread, 0.0).astype(BF16)


def sum_kernel(own, *refs):
    total = own[...]
    for ref in refs[:-1]:
        total = total + ref[...].astype(F32)
    refs[-1][...] = total.astype(BF16)


def update_kernel(panel, *refs):
    pieces, sends = refs[:-2], refs[-2:]
    parent = jnp.concatenate([piece[...] for piece in pieces], axis=1)
    down = lax.axis_index("row") % 2
    for send, slot in zip(sends, (1 - down, down)):
        send[...] = dot(parent, panel[slot]).astype(BF16)


def finish_kernel(red, skel, inv, interp, *refs):
    pieces, (red_out, ys_out) = refs[:-2], refs[-2:]
    parent = jnp.concatenate([piece[...] for piece in pieces], axis=1)
    count = parent.shape[1]
    xr = dot(parent, onehot(red[...], count)).astype(BF16)
    red_out[0] = dot_t(xr, inv[0])
    ys_out[0] = dot(parent, onehot(skel[...], count)) - dot_t(xr, interp[0])


def shards(
    rhs, skel1, red1, interp1, inv1, couple1, near1, skel2, red2, interp2, inv2, panel2, near2
):
    rows = lax.axis_size("row")
    row = lax.axis_index("row")
    groups, columns, total = rhs.shape
    redundant, block = interp1.shape[1:]
    skeletons = skel1.shape[1]
    width = groups * block
    s2_block, i2_block = interp2.shape[2], inv2.shape[2]
    red2_count = red2.shape[1]

    inverse = row_pieces(turned(inv1))[1:]
    hbm = pl.BlockSpec(memory_space=pltpu.HBM)
    inv1, interp1, couple1 = turned(inv1), turned(interp1), turned(couple1)
    xr1, ys1, couple1, own_inv1 = pl.pallas_call(
        pick_kernel,
        out_shape=(
            struct((groups, columns, redundant), BF16),
            struct((columns, width), F32),
            struct(couple1.shape, BF16),
            struct(inv1.shape, BF16),
        ),
        in_specs=[hbm] * 6,
        scratch_shapes=[
            pltpu.VMEM(rhs.shape, F32),
            pltpu.VMEM(red1.shape, jnp.int32),
            pltpu.VMEM(skel1.shape, jnp.int32),
            pltpu.VMEM(interp1.shape, BF16),
            pltpu.SemaphoreType.DMA((2 * groups + 4,)),
        ],
        compiler_params=pltpu.CompilerParams(vmem_limit_bytes=48 << 20),
    )(*(pltpu.with_memory_space_constraint(v, pltpu.HBM) for v in (rhs, red1, skel1, interp1, couple1, inv1)))

    vmem = pl.BlockSpec(memory_space=pltpu.VMEM)
    smem = pl.BlockSpec(memory_space=pltpu.SMEM)
    params = pltpu.CompilerParams(vmem_limit_bytes=48 << 20)
    send = struct((columns, width), BF16)
    own, *sends = pl.pallas_call(
        functools.partial(leaf_kernel, rows),
        out_shape=(struct((columns, width), F32),) + (send,) * len(SECTIONS),
        in_specs=[vmem] * (rows + 4),
        scratch_shapes=[
            pltpu.VMEM(((2 * REACH + 1) * groups + 1, columns, block), F32),
            pltpu.SMEM(near1.shape, jnp.int32),
            pltpu.SemaphoreType.DMA,
        ],
        compiler_params=params,
    )(near1, xr1, ys1, own_inv1, *inverse, couple1)

    arrived = [
        box_permute(piece, abs(section), section < 0) for piece, section in zip(sends, SECTIONS)
    ]

    place2 = functools.partial(
        shifted_index, half=row, block=block, groups=groups, skeletons=skeletons
    )
    red_place, skel_place = place2(red2), place2(
        lax.dynamic_slice_in_dim(skel2, row * s2_block, s2_block, 1)
    )
    red_one, panel_spread = pl.pallas_call(
        spread_kernel,
        out_shape=(
            struct((groups, columns, inv1.shape[1]), F32),
            struct((near2.shape[1], rows * width, s2_block), BF16),
        ),
        in_specs=[smem] + [vmem] * 4,
        compiler_params=params,
    )(near2, red_place, turned(panel2), xr1, own_inv1)
    own, panel_spread = lax.optimization_barrier((own, panel_spread))
    high = pl.pallas_call(sum_kernel, out_shape=send, compiler_params=params)(own, *arrived)
    pieces = row_pieces(high)
    updates = pl.pallas_call(
        update_kernel,
        out_shape=(struct((columns, s2_block), BF16),) * 2,
        compiler_params=params,
    )(panel_spread, *pieces)
    moved = [box_permute(piece, 1, flip) for piece, flip in zip(updates, (False, True))]
    red_two, ys2 = pl.pallas_call(
        finish_kernel,
        out_shape=(struct((1, columns, i2_block), F32), struct((1, columns, s2_block), F32)),
        compiler_params=params,
    )(red_place, skel_place, turned(inv2), turned(interp2), *pieces)
    skel_two = ys2 + moved[0].astype(F32)[None] + moved[1].astype(F32)[None]
    return red_one, red_two, skel_two


def solution(mesh):
    return jax.shard_map(
        shards,
        mesh=mesh,
        in_specs=(
            P("box", None, None),
            P("box", None),
            P("box", None),
            P("box", None, "row"),
            P("box", None, "row"),
            P("box", None, None, "row"),
            P("box", None),
            P("box", None),
            P("box", None),
            P("box", None, "row"),
            P("box", None, "row"),
            P("box", None, None, "row"),
            P("box", None),
        ),
        out_specs=(P("box", None, "row"), P("box", None, "row"), P("box", None, "row")),
        check_vma=False,
    )
```

```python
import functools

import jax
import jax.numpy as jnp
from jax import lax
from jax.experimental import pallas as pl
from jax.experimental.pallas import tpu as pltpu
from jax.sharding import PartitionSpec as P

F32 = jnp.float32
BF16 = jnp.bfloat16
REACH = 2


def row_pieces(block):
    rows = lax.axis_size("row")
    others = [
        lax.ppermute(block, "row", [(i, i ^ t) for i in range(rows)]) for t in range(1, rows)
    ]
    return [block] + others


def goes_up(box, distance, flip):
    return ((box // distance) % 2 == 0) != flip


def box_permute(block, distance, flip):
    boxes, rows = lax.axis_size("box"), lax.axis_size("row")
    route = []
    for box in range(boxes):
        target = box + (distance if goes_up(box, distance, flip) else -distance)
        inside = 0 <= target < boxes
        for row in range(rows):
            place = target * rows + row if inside else box * rows + (row ^ 1)
            route.append((box * rows + row, place))
    return lax.ppermute(block, ("box", "row"), route)


def onehot(index, count, dtype=BF16):
    spots = lax.broadcasted_iota(jnp.int32, (count, index.shape[1]), 0)
    return jnp.where(spots == index, 1.0, 0.0).astype(dtype)


def dot(a, b):
    return jnp.dot(a, b, preferred_element_type=F32)


def dot_t(a, b):
    return lax.dot_general(a, b, (((1,), (1,)), ((), ())), preferred_element_type=F32)


def turned(panel):
    return jnp.swapaxes(panel, -1, -2)


def own_part(values, block):
    row = lax.axis_index("row")
    chosen = values[:, :block]
    for place in range(1, values.shape[1] // block):
        part = values[:, place * block : (place + 1) * block]
        chosen = jnp.where(row == place, part, chosen)
    return chosen


def struct(shape, dtype):
    return jax.ShapeDtypeStruct(shape, dtype)


def pick_kernel(
    red, rhs, near, couple, inv,
    xr_out, rhs_out, near_out, couple_out, inv_out, red_in, spots, sems,
):
    groups, _, total = rhs.shape
    pairs = [(red, red_in)] + [(rhs.at[g], rhs_out.at[g]) for g in range(groups)]
    pairs += [(near, near_out), (inv, inv_out)]
    block = couple.shape[2]
    pairs += [(couple.at[g], couple_out.at[g, :, :block, :]) for g in range(groups)]
    copies = [
        pltpu.make_async_copy(source, held, sems.at[i]) for i, (source, held) in enumerate(pairs)
    ]
    for copy in copies:
        copy.start()
    copies[0].wait()
    for g in range(groups):
        spots[g] = onehot(red_in[g : g + 1, :], total)
    for copy in copies[1 : groups + 1]:
        copy.wait()
    for g in range(groups):
        xr_out[g] = dot(rhs_out[g].astype(BF16), spots[g]).astype(BF16)
    for copy in copies[groups + 1 :]:
        copy.wait()


def leaf_kernel(rows, block, near_held, xr, *refs):
    inv = refs[:rows]
    couple, own_out = refs[rows : rows + 2]
    sends = refs[rows + 2 : rows + 2 + len(ROUTES)]
    acc, near, sem = refs[-3:]
    fetch = pltpu.make_async_copy(near_held, near, sem)
    fetch.start()
    groups, slots = near.shape
    lanes = couple.shape[2]
    row = lax.axis_index("row")
    anchor = lax.axis_index("box")
    acc[...] = jnp.zeros_like(acc)
    leaves = []
    for g in range(groups):
        parts = [dot_t(xr[g], inv[t][g]) for t in range(rows)]
        placed = []
        for place in range(rows):
            chosen = parts[0]
            for t in range(1, rows):
                chosen = jnp.where(row == (place ^ t), parts[t], chosen)
            placed.append(chosen)
        leaves.append(jnp.concatenate(placed, axis=1).astype(BF16))
    fetch.wait()
    for g in range(groups):
        updates = dot_t(leaves[g], couple[g].reshape(slots * lanes, couple.shape[3]))
        for j in range(slots):
            target = near[g, j]
            clear = target - (anchor - REACH) * groups
            spot = jnp.where(target >= 0, clear, acc.shape[0] - 1)
            acc[spot] += updates[:, j * lanes : j * lanes + block]

    def merged(section):
        first = (section + REACH) * groups
        return jnp.concatenate([acc[first + g] for g in range(groups)], axis=1)

    own_out[...] = merged(0)
    for send, (distance, flip) in zip(sends, ROUTES):
        section = jnp.where(goes_up(anchor, distance, flip), distance, -distance)
        send[...] = merged(section).astype(BF16)


ROUTES = ((2, False), (1, True), (2, True), (1, False))


def shifted_index(index, half, block, groups, skeletons):
    child, place = index // skeletons, index % skeletons
    piece = (place // block) ^ half
    return piece * (groups * block) + child * block + place % block


def spread_kernel(near, red, panel, xr, inv1, rhs, skel, interp, red_out, ys_out, out):
    groups, columns, total = rhs.shape
    block = interp.shape[1]
    own = own_part(skel[...], block)
    for g in range(groups):
        red_out[g] = dot_t(xr[g], inv1[g])
        whole = rhs[g]
        high = whole.astype(BF16)
        low = (whole - high.astype(F32)).astype(BF16)
        both = dot(jnp.concatenate([high, low], axis=0), onehot(own[g : g + 1, :], total))
        ys = both[:columns] + both[columns:] - dot_t(xr[g], interp[g])
        ys_out[:, g * block : (g + 1) * block] = ys
    spots = onehot(red[...], out.shape[1])
    for slot in range(out.shape[0]):
        spread = dot_t(spots, panel[0, slot])
        out[slot] = jnp.where(near[0, slot] >= 0, spread, 0.0).astype(BF16)


def sum_kernel(own, *refs):
    total = own[...]
    for ref in refs[:-1]:
        total = total + ref[...].astype(F32)
    refs[-1][...] = total.astype(BF16)


def update_kernel(panel, *refs):
    pieces, sends = refs[:-2], refs[-2:]
    parent = jnp.concatenate([piece[...] for piece in pieces], axis=1)
    for send, flip in zip(sends, (True, False)):
        slot = jnp.where(goes_up(lax.axis_index("box"), 1, flip), 1, 0)
        send[...] = dot(parent, panel[slot]).astype(BF16)


def finish_kernel(red, skel, inv, interp, *refs):
    pieces, (red_out, ys_out) = refs[:-2], refs[-2:]
    parent = jnp.concatenate([piece[...] for piece in pieces], axis=1)
    count = parent.shape[1]
    xr = dot(parent, onehot(red[...], count)).astype(BF16)
    red_out[0] = dot_t(xr, inv[0])
    ys_out[0] = dot(parent, onehot(skel[...], count)) - dot_t(xr, interp[0])


def shards(
    rhs, skel1, red1, interp1, inv1, couple1, near1, skel2, red2, interp2, inv2, panel2, near2
):
    rows = lax.axis_size("row")
    row = lax.axis_index("row")
    groups, columns, total = rhs.shape
    redundant, block = interp1.shape[1:]
    skeletons = skel1.shape[1]
    width = groups * block
    s2_block, i2_block = interp2.shape[2], inv2.shape[2]
    red2_count = red2.shape[1]

    inverse = row_pieces(turned(inv1))[1:]
    vmem = pl.BlockSpec(memory_space=pltpu.VMEM)
    smem = pl.BlockSpec(memory_space=pltpu.SMEM)
    hbm = pl.BlockSpec(memory_space=pltpu.HBM)
    params = pltpu.CompilerParams(vmem_limit_bytes=48 << 20)
    inv1, couple1 = turned(inv1), turned(couple1)
    held = [pltpu.with_memory_space_constraint(v, pltpu.HBM) for v in (red1, rhs, near1, couple1, inv1)]
    lanes = -(-block // 128) * 128
    shapes = [v.shape for v in held[1:]]
    shapes[2] = shapes[2][:2] + (lanes, shapes[2][3])
    xr1, rhs, near1, couple1, own_inv1 = pl.pallas_call(
        pick_kernel,
        out_shape=(struct((groups, columns, redundant), BF16),)
        + tuple(struct(shape, v.dtype) for shape, v in zip(shapes, held[1:])),
        in_specs=[hbm] * 5,
        scratch_shapes=[
            pltpu.VMEM(red1.shape, jnp.int32),
            pltpu.VMEM((groups, total, redundant), BF16),
            pltpu.SemaphoreType.DMA((2 * groups + 3,)),
        ],
        compiler_params=params,
    )(*held)

    send = struct((columns, width), BF16)
    own, *sends = pl.pallas_call(
        functools.partial(leaf_kernel, rows, block),
        out_shape=(struct((columns, width), F32),) + (send,) * len(ROUTES),
        in_specs=[vmem] * (rows + 3),
        scratch_shapes=[
            pltpu.VMEM(((2 * REACH + 1) * groups + 1, columns, block), F32),
            pltpu.SMEM(near1.shape, jnp.int32),
            pltpu.SemaphoreType.DMA,
        ],
        compiler_params=params,
    )(near1, xr1, own_inv1, *inverse, couple1)

    arrived = [
        box_permute(piece, distance, flip) for piece, (distance, flip) in zip(sends, ROUTES)
    ]

    place2 = functools.partial(
        shifted_index, half=row, block=block, groups=groups, skeletons=skeletons
    )
    red_place, skel_place = place2(red2), place2(
        lax.dynamic_slice_in_dim(skel2, row * s2_block, s2_block, 1)
    )
    red_one, ys1, panel_spread = pl.pallas_call(
        spread_kernel,
        out_shape=(
            struct((groups, columns, inv1.shape[1]), F32),
            struct((columns, width), F32),
            struct((near2.shape[1], rows * width, s2_block), BF16),
        ),
        in_specs=[smem] + [vmem] * 7,
        compiler_params=params,
    )(near2, red_place, turned(panel2), xr1, own_inv1, rhs, skel1, turned(interp1))
    high = pl.pallas_call(sum_kernel, out_shape=send, compiler_params=params)(own, ys1, *arrived)
    pieces = row_pieces(high)
    updates = pl.pallas_call(
        update_kernel,
        out_shape=(struct((columns, s2_block), BF16),) * 2,
        compiler_params=params,
    )(panel_spread, *pieces)
    moved = [box_permute(piece, 1, flip) for piece, flip in zip(updates, (True, False))]
    red_two, ys2 = pl.pallas_call(
        finish_kernel,
        out_shape=(struct((1, columns, i2_block), F32), struct((1, columns, s2_block), F32)),
        compiler_params=params,
    )(red_place, skel_place, turned(inv2), turned(interp2), *pieces)
    skel_two = ys2 + moved[0].astype(F32)[None] + moved[1].astype(F32)[None]
    return red_one, red_two, skel_two


def solution(mesh):
    return jax.shard_map(
        shards,
        mesh=mesh,
        in_specs=(
            P("box", None, None),
            P("box", None),
            P("box", None),
            P("box", None, "row"),
            P("box", None, "row"),
            P("box", None, None, "row"),
            P("box", None),
            P("box", None),
            P("box", None),
            P("box", None, "row"),
            P("box", None, "row"),
            P("box", None, None, "row"),
            P("box", None),
        ),
        out_specs=(P("box", None, "row"), P("box", None, "row"), P("box", None, "row")),
        check_vma=False,
    )
```

```python
import functools

import jax
import jax.numpy as jnp
from jax import lax
from jax.experimental import pallas as pl
from jax.experimental.pallas import tpu as pltpu
from jax.sharding import PartitionSpec as P

F32 = jnp.float32
BF16 = jnp.bfloat16
REACH = 2


def row_pieces(block):
    rows = lax.axis_size("row")
    others = [
        lax.ppermute(block, "row", [(i, i ^ t) for i in range(rows)]) for t in range(1, rows)
    ]
    return [block] + others


def goes_up(box, distance, flip):
    return ((box // distance) % 2 == 0) != flip


def box_permute(block, distance, flip):
    boxes, rows = lax.axis_size("box"), lax.axis_size("row")
    route = []
    for box in range(boxes):
        target = box + (distance if goes_up(box, distance, flip) else -distance)
        inside = 0 <= target < boxes
        for row in range(rows):
            place = target * rows + row if inside else box * rows + (row ^ 1)
            route.append((box * rows + row, place))
    return lax.ppermute(block, ("box", "row"), route)


def onehot(index, count, dtype=BF16):
    spots = lax.broadcasted_iota(jnp.int32, (count, index.shape[1]), 0)
    return jnp.where(spots == index, 1.0, 0.0).astype(dtype)


def dot(a, b):
    return jnp.dot(a, b, preferred_element_type=F32)


def dot_t(a, b):
    return lax.dot_general(a, b, (((1,), (1,)), ((), ())), preferred_element_type=F32)


def turned(panel):
    return jnp.swapaxes(panel, -1, -2)


def own_part(values, block):
    row = lax.axis_index("row")
    chosen = values[:, :block]
    for place in range(1, values.shape[1] // block):
        part = values[:, place * block : (place + 1) * block]
        chosen = jnp.where(row == place, part, chosen)
    return chosen


def struct(shape, dtype):
    return jax.ShapeDtypeStruct(shape, dtype)


def pick_kernel(
    red, rhs, near, couple, inv,
    xr_out, rhs_out, near_out, couple_out, inv_out, red_in, spots, sems,
):
    groups, _, total = rhs.shape
    pairs = [(red, red_in)] + [(rhs.at[g], rhs_out.at[g]) for g in range(groups)]
    pairs += [(near, near_out), (inv, inv_out)]
    block = couple.shape[2]
    pairs += [(couple.at[g], couple_out.at[g, :, :block, :]) for g in range(groups)]
    copies = [
        pltpu.make_async_copy(source, held, sems.at[i]) for i, (source, held) in enumerate(pairs)
    ]
    for copy in copies:
        copy.start()
    copies[0].wait()
    for g in range(groups):
        spots[g] = onehot(red_in[g : g + 1, :], total)
    for copy in copies[1 : groups + 1]:
        copy.wait()
    for g in range(groups):
        xr_out[g] = dot(rhs_out[g].astype(BF16), spots[g]).astype(BF16)
    for copy in copies[groups + 1 :]:
        copy.wait()


def leaf_kernel(rows, block, near_held, xr, *refs):
    inv = refs[:rows]
    couple, own_out = refs[rows : rows + 2]
    sends = refs[rows + 2 : rows + 2 + len(ROUTES)]
    acc, near, sem = refs[-3:]
    fetch = pltpu.make_async_copy(near_held, near, sem)
    fetch.start()
    groups, slots = near.shape
    lanes = couple.shape[2]
    row = lax.axis_index("row")
    anchor = lax.axis_index("box")
    acc[...] = jnp.zeros_like(acc)
    leaves = []
    for g in range(groups):
        parts = [dot_t(xr[g], inv[t][g]) for t in range(rows)]
        placed = []
        for place in range(rows):
            chosen = parts[0]
            for t in range(1, rows):
                chosen = jnp.where(row == (place ^ t), parts[t], chosen)
            placed.append(chosen)
        leaves.append(jnp.concatenate(placed, axis=1).astype(BF16))
    fetch.wait()
    for g in range(groups):
        updates = dot_t(leaves[g], couple[g].reshape(slots * lanes, couple.shape[3]))
        for j in range(slots):
            target = near[g, j]
            clear = target - (anchor - REACH) * groups
            spot = jnp.where(target >= 0, clear, acc.shape[0] - 1)
            acc[spot] += updates[:, j * lanes : j * lanes + block]

    def merged(section):
        first = (section + REACH) * groups
        return jnp.concatenate([acc[first + g] for g in range(groups)], axis=1)

    own_out[...] = merged(0)
    for send, (distance, flip) in zip(sends, ROUTES):
        section = jnp.where(goes_up(anchor, distance, flip), distance, -distance)
        send[...] = merged(section).astype(BF16)


ROUTES = ((2, False), (1, True), (2, True), (1, False))


def shifted_index(index, half, block, groups, skeletons):
    child, place = index // skeletons, index % skeletons
    piece = (place // block) ^ half
    return piece * (groups * block) + child * block + place % block


def spread_kernel(near, red, panel, xr, inv1, rhs, skel, interp, red_out, ys_out, out):
    groups, columns, total = rhs.shape
    block = interp.shape[1]
    own = own_part(skel[...], block)
    for g in range(groups):
        red_out[g] = dot_t(xr[g], inv1[g])
        whole = rhs[g]
        high = whole.astype(BF16)
        low = (whole - high.astype(F32)).astype(BF16)
        both = dot(jnp.concatenate([high, low], axis=0), onehot(own[g : g + 1, :], total))
        ys = both[:columns] + both[columns:] - dot_t(xr[g], interp[g])
        ys_out[:, g * block : (g + 1) * block] = ys
    spots = onehot(red[...], out.shape[1])
    for slot in range(out.shape[0]):
        spread = dot_t(spots, panel[0, slot])
        out[slot] = jnp.where(near[0, slot] >= 0, spread, 0.0).astype(BF16)


def sum_kernel(own, *refs):
    total = own[...]
    for ref in refs[:-1]:
        total = total + ref[...].astype(F32)
    refs[-1][...] = total.astype(BF16)


def update_kernel(panel, *refs):
    pieces, sends = refs[:-2], refs[-2:]
    parent = jnp.concatenate([piece[...] for piece in pieces], axis=1)
    for send, flip in zip(sends, (True, False)):
        slot = jnp.where(goes_up(lax.axis_index("box"), 1, flip), 1, 0)
        send[...] = dot(parent, panel[slot]).astype(BF16)


def finish_kernel(red, skel, inv, interp, *refs):
    pieces, (red_out, ys_out) = refs[:-2], refs[-2:]
    parent = jnp.concatenate([piece[...] for piece in pieces], axis=1)
    count = parent.shape[1]
    xr = dot(parent, onehot(red[...], count)).astype(BF16)
    red_out[0] = dot_t(xr, inv[0])
    ys_out[0] = dot(parent, onehot(skel[...], count)) - dot_t(xr, interp[0])


def shards(
    rhs, skel1, red1, interp1, inv1, couple1, near1, skel2, red2, interp2, inv2, panel2, near2
):
    rows = lax.axis_size("row")
    row = lax.axis_index("row")
    groups, columns, total = rhs.shape
    redundant, block = interp1.shape[1:]
    skeletons = skel1.shape[1]
    width = groups * block
    s2_block, i2_block = interp2.shape[2], inv2.shape[2]
    red2_count = red2.shape[1]

    inverse = row_pieces(turned(inv1))[1:]
    vmem = pl.BlockSpec(memory_space=pltpu.VMEM)
    smem = pl.BlockSpec(memory_space=pltpu.SMEM)
    hbm = pl.BlockSpec(memory_space=pltpu.HBM)
    params = pltpu.CompilerParams(vmem_limit_bytes=48 << 20)
    inv1, couple1 = turned(inv1), turned(couple1)
    held = [pltpu.with_memory_space_constraint(v, pltpu.HBM) for v in (red1, rhs, near1, couple1, inv1)]
    lanes = -(-block // 128) * 128 if block % 16 == 0 else block
    shapes = [v.shape for v in held[1:]]
    shapes[2] = shapes[2][:2] + (lanes, shapes[2][3])
    xr1, rhs, near1, couple1, own_inv1 = pl.pallas_call(
        pick_kernel,
        out_shape=(struct((groups, columns, redundant), BF16),)
        + tuple(struct(shape, v.dtype) for shape, v in zip(shapes, held[1:])),
        in_specs=[hbm] * 5,
        scratch_shapes=[
            pltpu.VMEM(red1.shape, jnp.int32),
            pltpu.VMEM((groups, total, redundant), BF16),
            pltpu.SemaphoreType.DMA((2 * groups + 3,)),
        ],
        compiler_params=params,
    )(*held)

    send = struct((columns, width), BF16)
    own, *sends = pl.pallas_call(
        functools.partial(leaf_kernel, rows, block),
        out_shape=(struct((columns, width), F32),) + (send,) * len(ROUTES),
        in_specs=[vmem] * (rows + 3),
        scratch_shapes=[
            pltpu.VMEM(((2 * REACH + 1) * groups + 1, columns, block), F32),
            pltpu.SMEM(near1.shape, jnp.int32),
            pltpu.SemaphoreType.DMA,
        ],
        compiler_params=params,
    )(near1, xr1, own_inv1, *inverse, couple1)

    arrived = [
        box_permute(piece, distance, flip) for piece, (distance, flip) in zip(sends, ROUTES)
    ]

    place2 = functools.partial(
        shifted_index, half=row, block=block, groups=groups, skeletons=skeletons
    )
    red_place, skel_place = place2(red2), place2(
        lax.dynamic_slice_in_dim(skel2, row * s2_block, s2_block, 1)
    )
    red_one, ys1, panel_spread = pl.pallas_call(
        spread_kernel,
        out_shape=(
            struct((groups, columns, inv1.shape[1]), F32),
            struct((columns, width), F32),
            struct((near2.shape[1], rows * width, s2_block), BF16),
        ),
        in_specs=[smem] + [vmem] * 7,
        compiler_params=params,
    )(near2, red_place, turned(panel2), xr1, own_inv1, rhs, skel1, turned(interp1))
    high = pl.pallas_call(sum_kernel, out_shape=send, compiler_params=params)(own, ys1, *arrived)
    pieces = row_pieces(high)
    updates = pl.pallas_call(
        update_kernel,
        out_shape=(struct((columns, s2_block), BF16),) * 2,
        compiler_params=params,
    )(panel_spread, *pieces)
    moved = [box_permute(piece, 1, flip) for piece, flip in zip(updates, (True, False))]
    red_two, ys2 = pl.pallas_call(
        finish_kernel,
        out_shape=(struct((1, columns, i2_block), F32), struct((1, columns, s2_block), F32)),
        compiler_params=params,
    )(red_place, skel_place, turned(inv2), turned(interp2), *pieces)
    skel_two = ys2 + moved[0].astype(F32)[None] + moved[1].astype(F32)[None]
    return red_one, red_two, skel_two


def solution(mesh):
    return jax.shard_map(
        shards,
        mesh=mesh,
        in_specs=(
            P("box", None, None),
            P("box", None),
            P("box", None),
            P("box", None, "row"),
            P("box", None, "row"),
            P("box", None, None, "row"),
            P("box", None),
            P("box", None),
            P("box", None),
            P("box", None, "row"),
            P("box", None, "row"),
            P("box", None, None, "row"),
            P("box", None),
        ),
        out_specs=(P("box", None, "row"), P("box", None, "row"), P("box", None, "row")),
        check_vma=False,
    )
```

```python
import functools

import jax
import jax.numpy as jnp
from jax import lax
from jax.experimental import pallas as pl
from jax.experimental.pallas import tpu as pltpu
from jax.sharding import PartitionSpec as P

F32 = jnp.float32
BF16 = jnp.bfloat16
REACH = 2


def row_pieces(block):
    rows = lax.axis_size("row")
    others = [
        lax.ppermute(block, "row", [(i, i ^ t) for i in range(rows)]) for t in range(1, rows)
    ]
    return [block] + others


def goes_up(box, distance, flip):
    return ((box // distance) % 2 == 0) != flip


def box_permute(block, distance, flip):
    boxes, rows = lax.axis_size("box"), lax.axis_size("row")
    route = []
    for box in range(boxes):
        target = box + (distance if goes_up(box, distance, flip) else -distance)
        inside = 0 <= target < boxes
        for row in range(rows):
            place = target * rows + row if inside else box * rows + (row ^ 1)
            route.append((box * rows + row, place))
    return lax.ppermute(block, ("box", "row"), route)


def onehot(index, count, dtype=BF16):
    spots = lax.broadcasted_iota(jnp.int32, (count, index.shape[1]), 0)
    return jnp.where(spots == index, 1.0, 0.0).astype(dtype)


def dot(a, b):
    return jnp.dot(a, b, preferred_element_type=F32)


def dot_t(a, b):
    return lax.dot_general(a, b, (((1,), (1,)), ((), ())), preferred_element_type=F32)


def turned(panel):
    return jnp.swapaxes(panel, -1, -2)


def own_part(values, block):
    row = lax.axis_index("row")
    chosen = values[:, :block]
    for place in range(1, values.shape[1] // block):
        part = values[:, place * block : (place + 1) * block]
        chosen = jnp.where(row == place, part, chosen)
    return chosen


def struct(shape, dtype):
    return jax.ShapeDtypeStruct(shape, dtype)


def pick_kernel(
    red, rhs, near, couple, inv,
    xr_out, rhs_out, near_out, couple_out, inv_out, red_in, spots, sems,
):
    groups, _, total = rhs.shape
    pairs = [(red, red_in)] + [(rhs.at[g], rhs_out.at[g]) for g in range(groups)]
    pairs += [(near, near_out), (inv, inv_out)]
    block = couple.shape[2]
    pairs += [(couple.at[g], couple_out.at[g, :, :block, :]) for g in range(groups)]
    copies = [
        pltpu.make_async_copy(source, held, sems.at[i]) for i, (source, held) in enumerate(pairs)
    ]
    for copy in copies:
        copy.start()
    copies[0].wait()
    for g in range(groups):
        spots[g] = onehot(red_in[g : g + 1, :], total)
    for copy in copies[1 : groups + 1]:
        copy.wait()
    for g in range(groups):
        xr_out[g] = dot(rhs_out[g].astype(BF16), spots[g]).astype(BF16)
    for copy in copies[groups + 1 :]:
        copy.wait()


def leaf_kernel(rows, block, near_held, xr, *refs):
    inv = refs[:rows]
    couple, own_out = refs[rows : rows + 2]
    sends = refs[rows + 2 : rows + 2 + len(ROUTES)]
    acc, near, sem = refs[-3:]
    fetch = pltpu.make_async_copy(near_held, near, sem)
    fetch.start()
    groups, slots = near.shape
    lanes = couple.shape[2]
    row = lax.axis_index("row")
    anchor = lax.axis_index("box")
    acc[...] = jnp.zeros_like(acc)
    leaves = []
    for g in range(groups):
        parts = [dot_t(xr[g], inv[t][g]) for t in range(rows)]
        placed = []
        for place in range(rows):
            chosen = parts[0]
            for t in range(1, rows):
                chosen = jnp.where(row == (place ^ t), parts[t], chosen)
            placed.append(chosen)
        leaves.append(jnp.concatenate(placed, axis=1).astype(BF16))
    products = [
        dot_t(leaves[g], couple[g].reshape(slots * lanes, couple.shape[3])) for g in range(groups)
    ]
    fetch.wait()
    for g, updates in enumerate(products):
        for j in range(slots):
            target = near[g, j]
            clear = target - (anchor - REACH) * groups
            spot = jnp.where(target >= 0, clear, acc.shape[0] - 1)
            acc[spot] += updates[:, j * lanes : j * lanes + block]

    def merged(section):
        first = (section + REACH) * groups
        return jnp.concatenate([acc[first + g] for g in range(groups)], axis=1)

    own_out[...] = merged(0)
    for send, (distance, flip) in zip(sends, ROUTES):
        section = jnp.where(goes_up(anchor, distance, flip), distance, -distance)
        send[...] = merged(section).astype(BF16)


ROUTES = ((2, False), (1, True), (2, True), (1, False))


def shifted_index(index, half, block, groups, skeletons):
    child, place = index // skeletons, index % skeletons
    piece = (place // block) ^ half
    return piece * (groups * block) + child * block + place % block


def spread_kernel(near, red, panel, xr, inv1, rhs, skel, interp, red_out, ys_out, out):
    groups, columns, total = rhs.shape
    block = interp.shape[1]
    own = own_part(skel[...], block)
    for g in range(groups):
        red_out[g] = dot_t(xr[g], inv1[g])
        whole = rhs[g]
        high = whole.astype(BF16)
        low = (whole - high.astype(F32)).astype(BF16)
        both = dot(jnp.concatenate([high, low], axis=0), onehot(own[g : g + 1, :], total))
        ys = both[:columns] + both[columns:] - dot_t(xr[g], interp[g])
        ys_out[:, g * block : (g + 1) * block] = ys
    spots = onehot(red[...], out.shape[1])
    for slot in range(out.shape[0]):
        spread = dot_t(spots, panel[0, slot])
        out[slot] = jnp.where(near[0, slot] >= 0, spread, 0.0).astype(BF16)


def sum_kernel(own, *refs):
    total = own[...]
    for ref in refs[:-1]:
        total = total + ref[...].astype(F32)
    refs[-1][...] = total.astype(BF16)


def update_kernel(panel, *refs):
    pieces, first, sends = refs[:-4], refs[-4:-2], refs[-2:]
    width = pieces[0].shape[1]
    parent = jnp.concatenate([piece[...] for piece in pieces], axis=1)
    for begun, send, flip in zip(first, sends, (True, False)):
        slot = jnp.where(goes_up(lax.axis_index("box"), 1, flip), 1, 0)
        send[...] = (begun[...] + dot(parent, panel[slot, width:])).astype(BF16)


def own_update_kernel(panel, piece, *sends):
    for send, flip in zip(sends, (True, False)):
        slot = jnp.where(goes_up(lax.axis_index("box"), 1, flip), 1, 0)
        send[...] = dot(piece[...], panel[slot, : piece.shape[1]])


def finish_kernel(red, skel, inv, interp, *refs):
    pieces, (red_out, ys_out) = refs[:-2], refs[-2:]
    parent = jnp.concatenate([piece[...] for piece in pieces], axis=1)
    count = parent.shape[1]
    xr = dot(parent, onehot(red[...], count)).astype(BF16)
    red_out[0] = dot_t(xr, inv[0])
    ys_out[0] = dot(parent, onehot(skel[...], count)) - dot_t(xr, interp[0])


def shards(
    rhs, skel1, red1, interp1, inv1, couple1, near1, skel2, red2, interp2, inv2, panel2, near2
):
    rows = lax.axis_size("row")
    row = lax.axis_index("row")
    groups, columns, total = rhs.shape
    redundant, block = interp1.shape[1:]
    skeletons = skel1.shape[1]
    width = groups * block
    s2_block, i2_block = interp2.shape[2], inv2.shape[2]
    red2_count = red2.shape[1]

    inverse = row_pieces(turned(inv1))[1:]
    vmem = pl.BlockSpec(memory_space=pltpu.VMEM)
    smem = pl.BlockSpec(memory_space=pltpu.SMEM)
    hbm = pl.BlockSpec(memory_space=pltpu.HBM)
    params = pltpu.CompilerParams(vmem_limit_bytes=48 << 20)
    inv1, couple1 = turned(inv1), turned(couple1)
    held = [pltpu.with_memory_space_constraint(v, pltpu.HBM) for v in (red1, rhs, near1, couple1, inv1)]
    lanes = -(-block // 128) * 128 if block % 16 == 0 else block
    shapes = [v.shape for v in held[1:]]
    shapes[2] = shapes[2][:2] + (lanes, shapes[2][3])
    xr1, rhs, near1, couple1, own_inv1 = pl.pallas_call(
        pick_kernel,
        out_shape=(struct((groups, columns, redundant), BF16),)
        + tuple(struct(shape, v.dtype) for shape, v in zip(shapes, held[1:])),
        in_specs=[hbm] * 5,
        scratch_shapes=[
            pltpu.VMEM(red1.shape, jnp.int32),
            pltpu.VMEM((groups, total, redundant), BF16),
            pltpu.SemaphoreType.DMA((2 * groups + 3,)),
        ],
        compiler_params=params,
    )(*held)

    send = struct((columns, width), BF16)
    own, *sends = pl.pallas_call(
        functools.partial(leaf_kernel, rows, block),
        out_shape=(struct((columns, width), F32),) + (send,) * len(ROUTES),
        in_specs=[vmem] * (rows + 3),
        scratch_shapes=[
            pltpu.VMEM(((2 * REACH + 1) * groups + 1, columns, block), F32),
            pltpu.SMEM(near1.shape, jnp.int32),
            pltpu.SemaphoreType.DMA,
        ],
        compiler_params=params,
    )(near1, xr1, own_inv1, *inverse, couple1)

    panel2, inv2, interp2, interp1, skel1, red2, skel2, near2, _ = lax.optimization_barrier(
        (panel2, inv2, interp2, interp1, skel1, red2, skel2, near2, sends[0])
    )
    arrived = [
        box_permute(piece, distance, flip) for piece, (distance, flip) in zip(sends, ROUTES)
    ]

    place2 = functools.partial(
        shifted_index, half=row, block=block, groups=groups, skeletons=skeletons
    )
    red_place, skel_place = place2(red2), place2(
        lax.dynamic_slice_in_dim(skel2, row * s2_block, s2_block, 1)
    )
    red_one, ys1, panel_spread = pl.pallas_call(
        spread_kernel,
        out_shape=(
            struct((groups, columns, inv1.shape[1]), F32),
            struct((columns, width), F32),
            struct((near2.shape[1], rows * width, s2_block), BF16),
        ),
        in_specs=[smem] + [vmem] * 7,
        compiler_params=params,
    )(near2, red_place, turned(panel2), xr1, own_inv1, rhs, skel1, turned(interp1))
    high = pl.pallas_call(sum_kernel, out_shape=send, compiler_params=params)(own, ys1, *arrived)
    pieces = row_pieces(high)
    begun = pl.pallas_call(
        own_update_kernel,
        out_shape=(struct((columns, s2_block), F32),) * 2,
        compiler_params=params,
    )(panel_spread, pieces[0])
    updates = pl.pallas_call(
        update_kernel,
        out_shape=(struct((columns, s2_block), BF16),) * 2,
        compiler_params=params,
    )(panel_spread, *pieces[1:], *begun)
    moved = [box_permute(piece, 1, flip) for piece, flip in zip(updates, (True, False))]
    red_two, ys2 = pl.pallas_call(
        finish_kernel,
        out_shape=(struct((1, columns, i2_block), F32), struct((1, columns, s2_block), F32)),
        compiler_params=params,
    )(red_place, skel_place, turned(inv2), turned(interp2), *pieces)
    skel_two = ys2 + moved[0].astype(F32)[None] + moved[1].astype(F32)[None]
    return red_one, red_two, skel_two


def solution(mesh):
    return jax.shard_map(
        shards,
        mesh=mesh,
        in_specs=(
            P("box", None, None),
            P("box", None),
            P("box", None),
            P("box", None, "row"),
            P("box", None, "row"),
            P("box", None, None, "row"),
            P("box", None),
            P("box", None),
            P("box", None),
            P("box", None, "row"),
            P("box", None, "row"),
            P("box", None, None, "row"),
            P("box", None),
        ),
        out_specs=(P("box", None, "row"), P("box", None, "row"), P("box", None, "row")),
        check_vma=False,
    )
```

```python
import functools

import jax
import jax.numpy as jnp
from jax import lax
from jax.experimental import pallas as pl
from jax.experimental.pallas import tpu as pltpu
from jax.sharding import PartitionSpec as P

F32 = jnp.float32
BF16 = jnp.bfloat16
REACH = 2


def row_pieces(block):
    rows = lax.axis_size("row")
    others = [
        lax.ppermute(block, "row", [(i, i ^ t) for i in range(rows)]) for t in range(1, rows)
    ]
    return [block] + others


def goes_up(box, distance, flip):
    return ((box // distance) % 2 == 0) != flip


def box_permute(block, distance, flip):
    boxes, rows = lax.axis_size("box"), lax.axis_size("row")
    route = []
    for box in range(boxes):
        target = box + (distance if goes_up(box, distance, flip) else -distance)
        inside = 0 <= target < boxes
        for row in range(rows):
            place = target * rows + row if inside else box * rows + (row ^ 1)
            route.append((box * rows + row, place))
    return lax.ppermute(block, ("box", "row"), route)


def onehot(index, count, dtype=BF16):
    spots = lax.broadcasted_iota(jnp.int32, (count, index.shape[1]), 0)
    return jnp.where(spots == index, 1.0, 0.0).astype(dtype)


def dot(a, b):
    return jnp.dot(a, b, preferred_element_type=F32)


def dot_t(a, b):
    return lax.dot_general(a, b, (((1,), (1,)), ((), ())), preferred_element_type=F32)


def turned(panel):
    return jnp.swapaxes(panel, -1, -2)


def own_part(values, block):
    row = lax.axis_index("row")
    chosen = values[:, :block]
    for place in range(1, values.shape[1] // block):
        part = values[:, place * block : (place + 1) * block]
        chosen = jnp.where(row == place, part, chosen)
    return chosen


def struct(shape, dtype):
    return jax.ShapeDtypeStruct(shape, dtype)


def pick_kernel(
    red, rhs, near, couple, inv,
    xr_out, rhs_out, near_out, couple_out, inv_out, red_in, spots, sems,
):
    groups, _, total = rhs.shape
    pairs = [(red, red_in)] + [(rhs.at[g], rhs_out.at[g]) for g in range(groups)]
    pairs += [(near, near_out), (inv, inv_out)]
    block = couple.shape[2]
    pairs += [(couple.at[g], couple_out.at[g, :, :block, :]) for g in range(groups)]
    copies = [
        pltpu.make_async_copy(source, held, sems.at[i]) for i, (source, held) in enumerate(pairs)
    ]
    for copy in copies:
        copy.start()
    copies[0].wait()
    for g in range(groups):
        spots[g] = onehot(red_in[g : g + 1, :], total)
    for copy in copies[1 : groups + 1]:
        copy.wait()
    for g in range(groups):
        xr_out[g] = dot(rhs_out[g].astype(BF16), spots[g]).astype(BF16)
    for copy in copies[groups + 1 :]:
        copy.wait()


def leaf_kernel(rows, block, near_held, xr, *refs):
    inv = refs[:rows]
    couple, own_out = refs[rows : rows + 2]
    sends = refs[rows + 2 : rows + 2 + len(ROUTES)]
    acc, near, sem = refs[-3:]
    fetch = pltpu.make_async_copy(near_held, near, sem)
    fetch.start()
    groups, slots = near.shape
    lanes = couple.shape[2]
    row = lax.axis_index("row")
    anchor = lax.axis_index("box")
    acc[...] = jnp.zeros_like(acc)
    leaves = []
    for g in range(groups):
        parts = [dot_t(xr[g], inv[t][g]) for t in range(rows)]
        placed = []
        for place in range(rows):
            chosen = parts[0]
            for t in range(1, rows):
                chosen = jnp.where(row == (place ^ t), parts[t], chosen)
            placed.append(chosen)
        leaves.append(jnp.concatenate(placed, axis=1).astype(BF16))
    products = [
        dot_t(leaves[g], couple[g].reshape(slots * lanes, couple.shape[3])) for g in range(groups)
    ]
    fetch.wait()
    for g, updates in enumerate(products):
        for j in range(slots):
            target = near[g, j]
            clear = target - (anchor - REACH) * groups
            spot = jnp.where(target >= 0, clear, acc.shape[0] - 1)
            acc[spot] += updates[:, j * lanes : j * lanes + block]

    def merged(section):
        first = (section + REACH) * groups
        return jnp.concatenate([acc[first + g] for g in range(groups)], axis=1)

    own_out[...] = merged(0)
    for send, (distance, flip) in zip(sends, ROUTES):
        section = jnp.where(goes_up(anchor, distance, flip), distance, -distance)
        send[...] = merged(section).astype(BF16)


ROUTES = ((2, False), (1, True), (2, True), (1, False))


def shifted_index(index, half, block, groups, skeletons):
    child, place = index // skeletons, index % skeletons
    piece = (place // block) ^ half
    return piece * (groups * block) + child * block + place % block


def spread_kernel(near, red, panel, xr, inv1, rhs, skel, interp, red_out, ys_out, out):
    groups, columns, total = rhs.shape
    block = interp.shape[1]
    own = own_part(skel[...], block)
    for g in range(groups):
        red_out[g] = dot_t(xr[g], inv1[g])
        whole = rhs[g]
        high = whole.astype(BF16)
        low = (whole - high.astype(F32)).astype(BF16)
        both = dot(jnp.concatenate([high, low], axis=0), onehot(own[g : g + 1, :], total))
        ys = both[:columns] + both[columns:] - dot_t(xr[g], interp[g])
        ys_out[:, g * block : (g + 1) * block] = ys
    spots = onehot(red[...], out.shape[1])
    for slot in range(out.shape[0]):
        spread = dot_t(spots, panel[0, slot])
        out[slot] = jnp.where(near[0, slot] >= 0, spread, 0.0).astype(BF16)


def sum_kernel(own, *refs):
    total = own[...]
    for ref in refs[:-1]:
        total = total + ref[...].astype(F32)
    refs[-1][...] = total.astype(BF16)


def update_kernel(flip, panel, begun, *refs):
    pieces, send = refs[:-1], refs[-1]
    width = pieces[0].shape[1]
    parent = jnp.concatenate([piece[...] for piece in pieces], axis=1)
    slot = jnp.where(goes_up(lax.axis_index("box"), 1, flip), 1, 0)
    send[...] = (begun[...] + dot(parent, panel[slot, width:])).astype(BF16)


def own_update_kernel(panel, piece, *sends):
    for send, flip in zip(sends, (True, False)):
        slot = jnp.where(goes_up(lax.axis_index("box"), 1, flip), 1, 0)
        send[...] = dot(piece[...], panel[slot, : piece.shape[1]])


def finish_kernel(red, skel, inv, interp, *refs):
    pieces, (red_out, ys_out) = refs[:-2], refs[-2:]
    parent = jnp.concatenate([piece[...] for piece in pieces], axis=1)
    count = parent.shape[1]
    xr = dot(parent, onehot(red[...], count)).astype(BF16)
    red_out[0] = dot_t(xr, inv[0])
    ys_out[0] = dot(parent, onehot(skel[...], count)) - dot_t(xr, interp[0])


def shards(
    rhs, skel1, red1, interp1, inv1, couple1, near1, skel2, red2, interp2, inv2, panel2, near2
):
    rows = lax.axis_size("row")
    row = lax.axis_index("row")
    groups, columns, total = rhs.shape
    redundant, block = interp1.shape[1:]
    skeletons = skel1.shape[1]
    width = groups * block
    s2_block, i2_block = interp2.shape[2], inv2.shape[2]
    red2_count = red2.shape[1]

    inverse = row_pieces(turned(inv1))[1:]
    vmem = pl.BlockSpec(memory_space=pltpu.VMEM)
    smem = pl.BlockSpec(memory_space=pltpu.SMEM)
    hbm = pl.BlockSpec(memory_space=pltpu.HBM)
    params = pltpu.CompilerParams(vmem_limit_bytes=48 << 20)
    inv1, couple1 = turned(inv1), turned(couple1)
    held = [pltpu.with_memory_space_constraint(v, pltpu.HBM) for v in (red1, rhs, near1, couple1, inv1)]
    lanes = -(-block // 128) * 128 if block % 16 == 0 else block
    shapes = [v.shape for v in held[1:]]
    shapes[2] = shapes[2][:2] + (lanes, shapes[2][3])
    xr1, rhs, near1, couple1, own_inv1 = pl.pallas_call(
        pick_kernel,
        out_shape=(struct((groups, columns, redundant), BF16),)
        + tuple(struct(shape, v.dtype) for shape, v in zip(shapes, held[1:])),
        in_specs=[hbm] * 5,
        scratch_shapes=[
            pltpu.VMEM(red1.shape, jnp.int32),
            pltpu.VMEM((groups, total, redundant), BF16),
            pltpu.SemaphoreType.DMA((2 * groups + 3,)),
        ],
        compiler_params=params,
    )(*held)

    send = struct((columns, width), BF16)
    own, *sends = pl.pallas_call(
        functools.partial(leaf_kernel, rows, block),
        out_shape=(struct((columns, width), F32),) + (send,) * len(ROUTES),
        in_specs=[vmem] * (rows + 3),
        scratch_shapes=[
            pltpu.VMEM(((2 * REACH + 1) * groups + 1, columns, block), F32),
            pltpu.SMEM(near1.shape, jnp.int32),
            pltpu.SemaphoreType.DMA,
        ],
        compiler_params=params,
    )(near1, xr1, own_inv1, *inverse, couple1)

    panel2, inv2, interp2, interp1, skel1, red2, skel2, near2, _ = lax.optimization_barrier(
        (panel2, inv2, interp2, interp1, skel1, red2, skel2, near2, sends[0])
    )
    arrived = [
        box_permute(piece, distance, flip) for piece, (distance, flip) in zip(sends, ROUTES)
    ]

    place2 = functools.partial(
        shifted_index, half=row, block=block, groups=groups, skeletons=skeletons
    )
    red_place, skel_place = place2(red2), place2(
        lax.dynamic_slice_in_dim(skel2, row * s2_block, s2_block, 1)
    )
    red_one, ys1, panel_spread = pl.pallas_call(
        spread_kernel,
        out_shape=(
            struct((groups, columns, inv1.shape[1]), F32),
            struct((columns, width), F32),
            struct((near2.shape[1], rows * width, s2_block), BF16),
        ),
        in_specs=[smem] + [vmem] * 7,
        compiler_params=params,
    )(near2, red_place, turned(panel2), xr1, own_inv1, rhs, skel1, turned(interp1))
    high = pl.pallas_call(sum_kernel, out_shape=send, compiler_params=params)(own, ys1, *arrived)
    pieces = row_pieces(high)
    begun = pl.pallas_call(
        own_update_kernel,
        out_shape=(struct((columns, s2_block), F32),) * 2,
        compiler_params=params,
    )(panel_spread, pieces[0])
    moved = []
    for flip, part in zip((True, False), begun):
        update = pl.pallas_call(
            functools.partial(update_kernel, flip),
            out_shape=struct((columns, s2_block), BF16),
            compiler_params=params,
        )(panel_spread, part, *pieces[1:])
        moved.append(box_permute(update, 1, flip))
    red_two, ys2 = pl.pallas_call(
        finish_kernel,
        out_shape=(struct((1, columns, i2_block), F32), struct((1, columns, s2_block), F32)),
        compiler_params=params,
    )(red_place, skel_place, turned(inv2), turned(interp2), *pieces)
    skel_two = ys2 + moved[0].astype(F32)[None] + moved[1].astype(F32)[None]
    return red_one, red_two, skel_two


def solution(mesh):
    return jax.shard_map(
        shards,
        mesh=mesh,
        in_specs=(
            P("box", None, None),
            P("box", None),
            P("box", None),
            P("box", None, "row"),
            P("box", None, "row"),
            P("box", None, None, "row"),
            P("box", None),
            P("box", None),
            P("box", None),
            P("box", None, "row"),
            P("box", None, "row"),
            P("box", None, None, "row"),
            P("box", None),
        ),
        out_specs=(P("box", None, "row"), P("box", None, "row"), P("box", None, "row")),
        check_vma=False,
    )
```
